32 devices in a mesh: layer: 8 (over y, x, core), lat: 4 (over z).
Axes of the slice: x: 2, y: 2, z: 4, core: 2. Of those that a mesh axis runs over, the one named last changes fastest.
Arguments:
- inputs: bfloat16 [4, 128, 2048], P(None, None, 'lat'), may hold values from -6 to 6
- targets: bfloat16 [512, 2048], P(('layer', 'lat')), may hold values from -6 to 6
- top_index: int32 [4, 128, 64], replicated, may hold values from 0 to 8191, all different within a row
- enc_weight: bfloat16 [2048, 32768], P(None, ('layer', 'lat')), may hold values from -0.125 to 0.125
- dec_weight: bfloat16 [32768, 4, 2048], P(('layer', 'lat')), may hold values from -0.375 to 0.375
Outputs:
- errors: float32 [512, 2048], P(('layer', 'lat'))
- grad_enc: bfloat16 [2048, 32768], P(None, ('layer', 'lat'))
- grad_dec: bfloat16 [32768, 4, 2048], P(('layer', 'lat'))
The draws below stay inside these ranges and needn't reach their ends.
Inputs may be any that keep to these rules, and one draw needn't show every extreme that they name: `top_index`: each row names 64 different latents.
All inputs are finite; a program needn't handle non-finite values.
Results may differ from the reference program's by a relative error of at most 0.009.
Values may be sent and summed in bfloat16 or wider, within the bound.
A program may use at most 128 MiB of HBM per device.

```python
import jax
import jax.numpy as jnp
from jax import lax

D = 2048
F = 8192
K = 64
LAYERS = 4
TOK = 128


def block_levels(rng, extent, split, smallest, top_value):
    def one(position, blocks):
        steps = jax.random.uniform(jax.random.fold_in(jax.random.fold_in(rng, 6), position), (blocks,), jnp.float32, smallest / len(split), top_value / len(split))
        return jnp.repeat(jnp.exp(steps), extent[position] // blocks).reshape((-1,) + (1,) * (len(extent) - position - 1))

    gain = one(*split[0])
    for cut in split[1:]:
        gain = gain * one(*cut)
    return gain


def different_ones(key, rows, amount, top, lift):
    sequence = jax.random.permutation(jax.random.fold_in(key, 1), amount)
    pull = sequence
    for power in range(3):
        pull = pull * pull // amount
    pull = pull * lift // amount
    chance = jax.random.randint(jax.random.fold_in(key, 2), (rows, amount), 0, 4096) + pull
    holders = jax.random.permutation(jax.random.fold_in(key, 3), rows)[jnp.arange(amount) % rows]
    chance = jnp.where(jnp.arange(rows)[:, None] == holders[None, :], 1 << 14, chance)
    score = chance * amount + jnp.arange(amount)
    return lax.top_k(score.astype(jnp.int32), top)[1].astype(jnp.int32)


def normal_values(key, dims, deviation, limit, shards=(), kind=jnp.bfloat16):
    gain = block_levels(key, dims, shards, -0.22, 0.18) if shards else 1.0
    values = jax.random.normal(key, dims, jnp.float32) * deviation * gain
    return jnp.minimum(jnp.maximum(values, -limit), limit).astype(kind)


def setup_inputs(seed: int = 0) -> dict:
    keys = jax.random.split(jax.random.key(seed), 6)
    inputs = normal_values(keys[0], (LAYERS, TOK, D), 1.0, 6.0, ((2, 4),))
    targets = normal_values(keys[1], (LAYERS * TOK, D), 1.0, 6.0, ((0, 32),))
    top_index = different_ones(keys[2], LAYERS * TOK, F, K, 0).reshape((LAYERS, TOK, K))
    enc_weight = normal_values(keys[3], (D, LAYERS * F), D ** -0.5, 0.125, ((1, 32),))
    dec_weight = normal_values(keys[4], (LAYERS * F, LAYERS, D), (K * LAYERS) ** -0.5, 0.375, ((0, 32),))
    return dict(inputs=inputs, targets=targets, top_index=top_index, enc_weight=enc_weight, dec_weight=dec_weight)


def reference(inputs, targets, top_index, enc_weight, dec_weight):
    code_list = []
    active_list = []
    for source in range(LAYERS):
        preact = jnp.dot(inputs[source], enc_weight[:, source * F:(source + 1) * F], preferred_element_type=jnp.float32)
        token_ids = jnp.arange(TOK, dtype=jnp.int32)[:, None]
        active = jnp.zeros((TOK, F), jnp.float32).at[token_ids, top_index[source]].set(1.0)
        active_list.append(active)
        code_list.append((preact * active).astype(jnp.bfloat16))
    decoded_list = []
    for target in range(LAYERS):
        total = jnp.zeros((TOK, D), jnp.float32)
        for source in range(target + 1):
            total = total + jnp.dot(code_list[source], dec_weight[source * F:(source + 1) * F, target, :], preferred_element_type=jnp.float32)
        decoded_list.append(total)
    errors = jnp.concatenate(decoded_list, axis=0) - targets.astype(jnp.float32)
    err_b = errors.astype(jnp.bfloat16).reshape(LAYERS, TOK, D)
    enc_cols = []
    dec_rows = []
    for source in range(LAYERS):
        block = dec_weight[source * F:(source + 1) * F]
        code_grad = jnp.zeros((TOK, F), jnp.float32)
        per_target = []
        for target in range(LAYERS):
            if target >= source:
                code_grad = code_grad + jnp.dot(err_b[target], block[:, target, :].T, preferred_element_type=jnp.float32)
                per_target.append(jnp.dot(code_list[source].T, err_b[target], preferred_element_type=jnp.float32))
            else:
                per_target.append(jnp.zeros((F, D), jnp.float32))
        pre_grad = (code_grad * active_list[source]).astype(jnp.bfloat16)
        enc_cols.append(jnp.dot(inputs[source].T, pre_grad, preferred_element_type=jnp.float32).astype(jnp.bfloat16))
        dec_rows.append(jnp.stack(per_target, axis=1).astype(jnp.bfloat16))
    return errors, jnp.concatenate(enc_cols, axis=1), jnp.concatenate(dec_rows, axis=0)
```

```python
import functools

import jax
import jax.numpy as jnp
from jax import lax
from jax.experimental import pallas as pl
from jax.experimental.pallas import tpu as pltpu
from jax.sharding import PartitionSpec as P

BF = jnp.bfloat16
F32 = jnp.float32
CHUNKS = 2


def exchange_kernel(n_t, n_lat, part, targets, errors, all_err,
                    sib_rx, q, xy_rx, zs, z_rx,
                    s1, r1, s2, r2, s3, r3, s4, r4, s5, r5, s6, r6):
    row = lax.axis_index("layer")
    z = lax.axis_index("lat")
    s = row // 2
    c = row % 2
    width = part.shape[2]
    half = part.shape[1] // 2
    rows = half // n_lat
    cw = width // CHUNKS
    sibling = (s * 2 + 1 - c, z)
    mine = pl.ds(pl.multiple_of(c * half, half), half)
    other = pl.ds(pl.multiple_of((1 - c) * half, half), half)

    def col(t):
        return (2 * t + c, z)

    def lat(zz):
        return (row, zz)

    def cols(ch):
        return pl.ds(ch * cw, cw)

    def rblock(zz):
        return pl.ds(pl.multiple_of(zz * rows, rows), rows)

    def eblock(zz):
        return pl.ds(pl.multiple_of(c * half + zz * rows, rows), rows)

    def copy(src, dst, ssem, rsem, dev):
        return pltpu.make_async_remote_copy(
            src_ref=src, dst_ref=dst, send_sem=ssem, recv_sem=rsem,
            device_id=dev, device_id_type=pl.DeviceIdType.MESH)

    barrier = pltpu.get_barrier_semaphore()
    pl.semaphore_signal(barrier, inc=1, device_id=sibling, device_id_type=pl.DeviceIdType.MESH)
    for t in range(n_t):
        @pl.when(t != s)
        def _():
            pl.semaphore_signal(barrier, inc=1, device_id=col(t), device_id_type=pl.DeviceIdType.MESH)
    for zz in range(n_lat):
        @pl.when(zz != z)
        def _():
            pl.semaphore_signal(barrier, inc=1, device_id=lat(zz), device_id_type=pl.DeviceIdType.MESH)
    pl.semaphore_wait(barrier, n_t + n_lat - 1)

    def pair(ch, t):
        return copy(part.at[t, other, cols(ch)], sib_rx.at[t, :, cols(ch)],
                    s1.at[ch, t], r1.at[ch, t], sibling)

    def to_target(ch, t):
        return copy(q.at[t, :, cols(ch)], xy_rx.at[s, :, cols(ch)],
                    s2.at[ch, t], r2.at[ch, s], col(t))

    def from_source(ch, ss):
        return copy(q.at[ss, :, cols(ch)], xy_rx.at[ss, :, cols(ch)],
                    s2.at[ch, ss], r2.at[ch, ss], col(ss))

    def to_lat(ch, zz):
        return copy(zs.at[rblock(zz), cols(ch)], z_rx.at[z, :, cols(ch)],
                    s3.at[ch, zz], r3.at[ch, z], lat(zz))

    def from_lat(ch, zz):
        return copy(zs.at[rblock(zz), cols(ch)], z_rx.at[zz, :, cols(ch)],
                    s3.at[ch, zz], r3.at[ch, zz], lat(zz))

    def err_to_lat(ch, zz):
        return copy(all_err.at[s, eblock(z), cols(ch)], all_err.at[s, eblock(z), cols(ch)],
                    s4.at[ch, zz], r4.at[ch, z], lat(zz))

    def err_from_lat(ch, zz):
        return copy(all_err.at[s, eblock(zz), cols(ch)], all_err.at[s, eblock(zz), cols(ch)],
                    s4.at[ch, zz], r4.at[ch, zz], lat(zz))

    def err_to_source(ch, ss):
        return copy(all_err.at[s, mine, cols(ch)], all_err.at[s, mine, cols(ch)],
                    s5.at[ch, ss], r5.at[ch, s], col(ss))

    def err_from_target(ch, t):
        return copy(all_err.at[t, mine, cols(ch)], all_err.at[t, mine, cols(ch)],
                    s5.at[ch, t], r5.at[ch, t], col(t))

    def err_pair(ch, t):
        return copy(all_err.at[t, mine, cols(ch)], all_err.at[t, mine, cols(ch)],
                    s6.at[ch, t], r6.at[ch, t], sibling)

    def err_pair_in(ch, t):
        return copy(all_err.at[t, other, cols(ch)], all_err.at[t, other, cols(ch)],
                    s6.at[ch, t], r6.at[ch, t], sibling)

    for ch in range(CHUNKS):
        for t in reversed(range(n_t)):
            @pl.when(t >= s)
            def _():
                pair(ch, t).start()
    for t in range(n_t):
        @pl.when(t < s)
        def _():
            all_err[t] = jnp.zeros((2 * half, width), BF)
    for ch in range(CHUNKS):
        for t in reversed(range(n_t)):
            @pl.when(t >= s)
            def _():
                pair(ch, t).wait_recv()

            @pl.when(t > s)
            def _():
                q[t, :, cols(ch)] = (part[t, mine, cols(ch)].astype(F32)
                                     + sib_rx[t, :, cols(ch)].astype(F32)).astype(BF)
                to_target(ch, t).start()
    for ch in range(CHUNKS):
        for ss in range(n_t):
            @pl.when(ss == s)
            def _():
                total = (part[ss, mine, cols(ch)].astype(F32)
                         + sib_rx[ss, :, cols(ch)].astype(F32))
                for src in range(ss):
                    from_source(ch, src).wait_recv()
                    total = total + xy_rx[src, :, cols(ch)].astype(F32)
                zs[:, cols(ch)] = total.astype(BF)
        for zz in range(n_lat):
            @pl.when(zz != z)
            def _():
                to_lat(ch, zz).start()
    for ch in range(CHUNKS):
        z_rx[z, :, cols(ch)] = zs[rblock(z), cols(ch)]
        for zz in range(n_lat):
            @pl.when(zz != z)
            def _():
                from_lat(ch, zz).wait_recv()
        total = z_rx[0, :, cols(ch)].astype(F32)
        for zz in range(1, n_lat):
            total = total + z_rx[zz, :, cols(ch)].astype(F32)
        err = total - targets[:, cols(ch)].astype(F32)
        errors[:, cols(ch)] = err
        all_err[s, eblock(z), cols(ch)] = err.astype(BF)
        for zz in range(n_lat):
            @pl.when(zz != z)
            def _():
                err_to_lat(ch, zz).start()
    for ch in range(CHUNKS):
        for zz in range(n_lat):
            @pl.when(zz != z)
            def _():
                err_from_lat(ch, zz).wait_recv()
        for ss in range(n_t):
            @pl.when(ss < s)
            def _():
                err_to_source(ch, ss).start()
        err_pair(ch, s).start()
    for ch in range(CHUNKS):
        for t in range(n_t):
            @pl.when(t > s)
            def _():
                err_from_target(ch, t).wait_recv()
                err_pair(ch, t).start()
    for ch in range(CHUNKS):
        for t in range(n_t):
            @pl.when(t >= s)
            def _():
                err_pair_in(ch, t).wait_recv()
                err_pair(ch, t).wait_send()
                pair(ch, t).wait_send()

            @pl.when(t > s)
            def _():
                to_target(ch, t).wait_send()

            @pl.when(t < s)
            def _():
                err_to_source(ch, t).wait_send()
        for zz in range(n_lat):
            @pl.when(zz != z)
            def _():
                to_lat(ch, zz).wait_send()
                err_to_lat(ch, zz).wait_send()


def exchange(part, targets):
    n_t, tok, width = part.shape
    n_lat = lax.axis_size("lat")
    half = tok // 2
    rows = half // n_lat
    vm = pl.BlockSpec(memory_space=pltpu.VMEM)
    dma = pltpu.SemaphoreType.DMA
    sems = []
    for n in (n_t, n_t, n_lat, n_lat, n_t, n_t):
        sems += [dma((CHUNKS, n)), dma((CHUNKS, n))]
    return pl.pallas_call(
        functools.partial(exchange_kernel, n_t, n_lat),
        out_shape=(jax.ShapeDtypeStruct((rows, width), F32),
                   jax.ShapeDtypeStruct((n_t, tok, width), BF)),
        in_specs=[vm, vm],
        out_specs=(vm, vm),
        scratch_shapes=[
            pltpu.VMEM((n_t, half, width), BF),
            pltpu.VMEM((n_t, half, width), BF),
            pltpu.VMEM((n_t, half, width), BF),
            pltpu.VMEM((half, width), BF),
            pltpu.VMEM((n_lat, rows, width), BF),
        ] + sems,
        compiler_params=pltpu.CompilerParams(
            collective_id=0, has_side_effects=True, vmem_limit_bytes=24 * 2**20),
        cost_estimate=pl.CostEstimate(flops=2**24, bytes_accessed=2**24, transcendentals=0),
    )(part, targets)


def per_device(inputs, targets, top_index, enc_weight, dec_weight):
    n_layer = lax.axis_size("layer")
    n_lat = lax.axis_size("lat")
    layer_count = inputs.shape[0]
    tok_count = inputs.shape[1]
    lat_dev = enc_weight.shape[1]
    per_layer = n_layer // layer_count
    layer_id = lax.axis_index("layer") // per_layer
    lat_first = (lax.axis_index("layer") % per_layer * n_lat + lax.axis_index("lat")) * lat_dev
    own_part = lax.dynamic_index_in_dim(inputs, layer_id, 0, keepdims=False)
    features = lax.all_gather(own_part, "lat", axis=1, tiled=True)
    preact = jnp.dot(features, enc_weight, preferred_element_type=jnp.float32)
    chosen = lax.dynamic_index_in_dim(top_index, layer_id, 0, keepdims=False)
    lat_ids = lat_first + jnp.arange(lat_dev, dtype=jnp.int32)
    active = jnp.any(chosen[:, :, None] == lat_ids[None, None, :], axis=1).astype(jnp.float32)
    code_vals = (preact * active).astype(jnp.bfloat16)
    reach_mask = (jnp.arange(layer_count, dtype=jnp.int32) >= layer_id).astype(jnp.float32)
    width = dec_weight.shape[2]
    row_count = targets.shape[0] * lax.axis_size(("layer", "lat"))
    result = jnp.einsum("nf,ftd->tnd", code_vals, dec_weight, preferred_element_type=jnp.float32)
    if per_layer == 2 and targets.shape[0] * 2 * n_lat == tok_count and targets.shape[0] % 16 == 0:
        errors, err_used = exchange(result.astype(BF), targets)
    else:
        result = result * reach_mask[:, None, None]
        decoded = lax.psum_scatter(
            result.reshape(row_count, width), ("layer", "lat"), scatter_dimension=0, tiled=True
        )
        errors = decoded - targets.astype(jnp.float32)
        err_b = errors.astype(jnp.bfloat16)
        all_err = lax.all_gather(err_b, ("layer", "lat"), axis=0, tiled=True)
        err_used = (
            all_err.reshape(layer_count, tok_count, width)
            * reach_mask.astype(jnp.bfloat16)[:, None, None]
        )
    code_grad = jnp.einsum("lnd,fld->nf", err_used, dec_weight, preferred_element_type=jnp.float32)
    pre_grad = (code_grad * active).astype(jnp.bfloat16)
    grad_enc = lax.dot_general(
        features, pre_grad, (((0,), (0,)), ((), ())), preferred_element_type=jnp.float32
    ).astype(jnp.bfloat16)
    grad_dec = jnp.einsum(
        "nf,lnd->fld", code_vals, err_used, preferred_element_type=jnp.float32
    ).astype(jnp.bfloat16)
    return (errors, grad_enc, grad_dec)


def solution(mesh):
    in_specs = (
        P(None, None, "lat"),
        P(("layer", "lat"), None),
        P(),
        P(None, ("layer", "lat")),
        P(("layer", "lat"), None, None),
    )
    out_specs = (
        P(("layer", "lat"), None),
        P(None, ("layer", "lat")),
        P(("layer", "lat"), None, None),
    )
    return jax.shard_map(
        per_device, mesh=mesh, in_specs=in_specs, out_specs=out_specs, check_vma=False
    )
```

```python
import functools

import jax
import jax.numpy as jnp
from jax import lax
from jax.experimental import pallas as pl
from jax.experimental.pallas import tpu as pltpu
from jax.sharding import PartitionSpec as P

BF = jnp.bfloat16
F32 = jnp.float32
CHUNKS = 2


def exchange_kernel(n_t, n_lat, part, targets, errors, all_err,
                    sib_rx, q, xy_rx, zs, z_rx,
                    s1, r1, s2, r2, s3, r3, s4, r4, s5, r5, s6, r6):
    row = lax.axis_index("layer")
    z = lax.axis_index("lat")
    s = row // 2
    c = row % 2
    width = part.shape[2]
    half = part.shape[1] // 2
    rows = half // n_lat
    cw = width // CHUNKS
    sibling = (s * 2 + 1 - c, z)
    mine = pl.ds(pl.multiple_of(c * half, half), half)
    other = pl.ds(pl.multiple_of((1 - c) * half, half), half)

    def col(t):
        return (2 * t + c, z)

    def lat(zz):
        return (row, zz)

    def cols(ch):
        return pl.ds(ch * cw, cw)

    def rblock(zz):
        return pl.ds(pl.multiple_of(zz * rows, rows), rows)

    def eblock(zz):
        return pl.ds(pl.multiple_of(c * half + zz * rows, rows), rows)

    def copy(src, dst, ssem, rsem, dev):
        return pltpu.make_async_remote_copy(
            src_ref=src, dst_ref=dst, send_sem=ssem, recv_sem=rsem,
            device_id=dev, device_id_type=pl.DeviceIdType.MESH)

    barrier = pltpu.get_barrier_semaphore()
    pl.semaphore_signal(barrier, inc=1, device_id=sibling, device_id_type=pl.DeviceIdType.MESH)
    for t in range(n_t):
        @pl.when(t != s)
        def _():
            pl.semaphore_signal(barrier, inc=1, device_id=col(t), device_id_type=pl.DeviceIdType.MESH)
    for zz in range(n_lat):
        @pl.when(zz != z)
        def _():
            pl.semaphore_signal(barrier, inc=1, device_id=lat(zz), device_id_type=pl.DeviceIdType.MESH)
    pl.semaphore_wait(barrier, n_t + n_lat - 1)

    def pair(ch, t):
        return copy(part.at[t, other, cols(ch)], sib_rx.at[t, :, cols(ch)],
                    s1.at[ch, t], r1.at[ch, t], sibling)

    def to_target(ch, t):
        return copy(q.at[t, :, cols(ch)], xy_rx.at[s, :, cols(ch)],
                    s2.at[ch, t], r2.at[ch, s], col(t))

    def from_source(ch, ss):
        return copy(q.at[ss, :, cols(ch)], xy_rx.at[ss, :, cols(ch)],
                    s2.at[ch, ss], r2.at[ch, ss], col(ss))

    def to_lat(ch, zz):
        return copy(zs.at[rblock(zz), cols(ch)], z_rx.at[z, :, cols(ch)],
                    s3.at[ch, zz], r3.at[ch, z], lat(zz))

    def from_lat(ch, zz):
        return copy(zs.at[rblock(zz), cols(ch)], z_rx.at[zz, :, cols(ch)],
                    s3.at[ch, zz], r3.at[ch, zz], lat(zz))

    def err_to_lat(ch, zz):
        return copy(all_err.at[s, eblock(z), cols(ch)], all_err.at[s, eblock(z), cols(ch)],
                    s4.at[ch, zz], r4.at[ch, z], lat(zz))

    def err_from_lat(ch, zz):
        return copy(all_err.at[s, eblock(zz), cols(ch)], all_err.at[s, eblock(zz), cols(ch)],
                    s4.at[ch, zz], r4.at[ch, zz], lat(zz))

    def err_to_source(ch, ss):
        return copy(all_err.at[s, mine, cols(ch)], all_err.at[s, mine, cols(ch)],
                    s5.at[ch, ss], r5.at[ch, s], col(ss))

    def err_from_target(ch, t):
        return copy(all_err.at[t, mine, cols(ch)], all_err.at[t, mine, cols(ch)],
                    s5.at[ch, t], r5.at[ch, t], col(t))

    def err_pair(ch, t):
        return copy(all_err.at[t, mine, cols(ch)], all_err.at[t, mine, cols(ch)],
                    s6.at[ch, t], r6.at[ch, t], sibling)

    def err_pair_in(ch, t):
        return copy(all_err.at[t, other, cols(ch)], all_err.at[t, other, cols(ch)],
                    s6.at[ch, t], r6.at[ch, t], sibling)

    for ch in range(CHUNKS):
        for t in reversed(range(n_t)):
            @pl.when(t >= s)
            def _():
                pair(ch, t).start()
    for t in range(n_t):
        @pl.when(t < s)
        def _():
            all_err[t] = jnp.zeros((2 * half, width), BF)
    for ch in range(CHUNKS):
        for t in reversed(range(n_t)):
            @pl.when(t >= s)
            def _():
                pair(ch, t).wait_recv()

            @pl.when(t > s)
            def _():
                q[t, :, cols(ch)] = (part[t, mine, cols(ch)].astype(F32)
                                     + sib_rx[t, :, cols(ch)].astype(F32)).astype(BF)
                to_target(ch, t).start()
    for ch in range(CHUNKS):
        for ss in range(n_t):
            @pl.when(ss == s)
            def _():
                total = (part[ss, mine, cols(ch)].astype(F32)
                         + sib_rx[ss, :, cols(ch)].astype(F32))
                for src in range(ss):
                    from_source(ch, src).wait_recv()
                    total = total + xy_rx[src, :, cols(ch)].astype(F32)
                zs[:, cols(ch)] = total.astype(BF)
        for zz in range(n_lat):
            @pl.when(zz != z)
            def _():
                to_lat(ch, zz).start()
    for ch in range(CHUNKS):
        z_rx[z, :, cols(ch)] = zs[rblock(z), cols(ch)]
        for zz in range(n_lat):
            @pl.when(zz != z)
            def _():
                from_lat(ch, zz).wait_recv()
        total = z_rx[0, :, cols(ch)].astype(F32)
        for zz in range(1, n_lat):
            total = total + z_rx[zz, :, cols(ch)].astype(F32)
        err = total - targets[:, cols(ch)].astype(F32)
        errors[:, cols(ch)] = err
        all_err[s, eblock(z), cols(ch)] = err.astype(BF)
        for zz in range(n_lat):
            @pl.when(zz != z)
            def _():
                err_to_lat(ch, zz).start()
    for ch in range(CHUNKS):
        for zz in range(n_lat):
            @pl.when(zz != z)
            def _():
                err_from_lat(ch, zz).wait_recv()
        for ss in range(n_t):
            @pl.when(ss < s)
            def _():
                err_to_source(ch, ss).start()
        err_pair(ch, s).start()
    for ch in range(CHUNKS):
        for t in range(n_t):
            @pl.when(t > s)
            def _():
                err_from_target(ch, t).wait_recv()
                err_pair(ch, t).start()
    for ch in range(CHUNKS):
        for t in range(n_t):
            @pl.when(t >= s)
            def _():
                err_pair_in(ch, t).wait_recv()
                err_pair(ch, t).wait_send()
                pair(ch, t).wait_send()

            @pl.when(t > s)
            def _():
                to_target(ch, t).wait_send()

            @pl.when(t < s)
            def _():
                err_to_source(ch, t).wait_send()
        for zz in range(n_lat):
            @pl.when(zz != z)
            def _():
                to_lat(ch, zz).wait_send()
                err_to_lat(ch, zz).wait_send()


def exchange(part, targets):
    n_t, tok, width = part.shape
    n_lat = lax.axis_size("lat")
    half = tok // 2
    rows = half // n_lat
    vm = pl.BlockSpec(memory_space=pltpu.VMEM)
    dma = pltpu.SemaphoreType.DMA
    sems = []
    for n in (n_t, n_t, n_lat, n_lat, n_t, n_t):
        sems += [dma((CHUNKS, n)), dma((CHUNKS, n))]
    return pl.pallas_call(
        functools.partial(exchange_kernel, n_t, n_lat),
        out_shape=(jax.ShapeDtypeStruct((rows, width), F32),
                   jax.ShapeDtypeStruct((n_t, tok, width), BF)),
        in_specs=[vm, vm],
        out_specs=(vm, vm),
        scratch_shapes=[
            pltpu.VMEM((n_t, half, width), BF),
            pltpu.VMEM((n_t, half, width), BF),
            pltpu.VMEM((n_t, half, width), BF),
            pltpu.VMEM((half, width), BF),
            pltpu.VMEM((n_lat, rows, width), BF),
        ] + sems,
        compiler_params=pltpu.CompilerParams(
            collective_id=0, has_side_effects=True, vmem_limit_bytes=24 * 2**20),
        cost_estimate=pl.CostEstimate(flops=2**24, bytes_accessed=2**24, transcendentals=0),
    )(part, targets)


def gather_kernel(n_lat, own, feat, s1, r1, s2, r2):
    row = lax.axis_index("layer")
    z = lax.axis_index("lat")
    s = row // 2
    c = row % 2
    cut = own.shape[2]
    piece = cut // 2
    sibling = (s * 2 + 1 - c, z)
    mesh_id = pl.DeviceIdType.MESH

    def cols(zz, cc):
        return pl.ds(pl.multiple_of(zz * cut + cc * piece, piece), piece)

    barrier = pltpu.get_barrier_semaphore()
    pl.semaphore_signal(barrier, inc=1, device_id=sibling, device_id_type=mesh_id)
    for zz in range(n_lat):
        @pl.when(zz != z)
        def _():
            pl.semaphore_signal(barrier, inc=1, device_id=(row, zz), device_id_type=mesh_id)
    pl.semaphore_wait(barrier, n_lat)

    def send(zz):
        return pltpu.make_async_remote_copy(
            src_ref=own.at[s, :, pl.ds(pl.multiple_of(c * piece, piece), piece)],
            dst_ref=feat.at[:, cols(z, c)], send_sem=s1.at[zz], recv_sem=r1.at[z],
            device_id=(row, zz), device_id_type=mesh_id)

    def arrive(zz):
        return pltpu.make_async_remote_copy(
            src_ref=feat.at[:, cols(zz, c)],
            dst_ref=feat.at[:, cols(zz, c)], send_sem=s1.at[zz], recv_sem=r1.at[zz],
            device_id=(row, zz), device_id_type=mesh_id)

    def forward(zz, cc):
        return pltpu.make_async_remote_copy(
            src_ref=feat.at[:, cols(zz, cc)],
            dst_ref=feat.at[:, cols(zz, cc)], send_sem=s2.at[zz], recv_sem=r2.at[zz],
            device_id=sibling, device_id_type=mesh_id)

    for zz in range(n_lat):
        @pl.when(zz != z)
        def _():
            send(zz).start()
    feat[:, pl.ds(pl.multiple_of(z * cut, cut), cut)] = own[s]
    for zz in range(n_lat):
        @pl.when(zz != z)
        def _():
            arrive(zz).wait_recv()
            forward(zz, c).start()
    for zz in range(n_lat):
        @pl.when(zz != z)
        def _():
            forward(zz, 1 - c).wait_recv()
            forward(zz, c).wait_send()
            send(zz).wait_send()


def gather_features(inputs):
    n_lat = lax.axis_size("lat")
    _, tok, cut = inputs.shape
    vm = pl.BlockSpec(memory_space=pltpu.VMEM)
    dma = pltpu.SemaphoreType.DMA((n_lat,))
    return pl.pallas_call(
        functools.partial(gather_kernel, n_lat),
        out_shape=jax.ShapeDtypeStruct((tok, cut * n_lat), BF),
        in_specs=[vm],
        out_specs=vm,
        scratch_shapes=[dma, dma, dma, dma],
        compiler_params=pltpu.CompilerParams(
            collective_id=1, has_side_effects=True, vmem_limit_bytes=4 * 2**20),
        cost_estimate=pl.CostEstimate(flops=2**20, bytes_accessed=2**21, transcendentals=0),
    )(inputs)


def spread_matrix(fb, n_t):
    f = lax.broadcasted_iota(jnp.int32, (fb, fb * n_t), 0)
    q = lax.broadcasted_iota(jnp.int32, (fb, fb * n_t), 1)
    return ((q >= f * n_t) & (q < (f + 1) * n_t)).astype(F32).astype(BF)


def load_copies(dec, xin, sem, block, fb):
    rows = pl.ds(block * fb, fb)
    return [pltpu.make_async_copy(dec.at[rows, :, pl.ds(j * 128, 128)],
                                  xin.at[j, rows], sem.at[block, j])
            for j in range(xin.shape[0])]


def wide(ref, first, count, block, fb):
    n_t = ref.shape[2]
    parts = [ref.at[first + j, pl.ds(block * fb, fb)].reshape(fb * n_t, 128)[...]
             for j in range(count)]
    return jnp.concatenate(parts, axis=1)


GROUP = 4


def decode_kernel(fb, n_blocks, feat, chosen, ids, enc, dec, part, codes, active,
                  xin, acc, lhs, spread, sem):
    n_t, tok, width = part.shape
    for b in range(n_blocks):
        for cp in load_copies(dec, xin, sem, b, fb):
            cp.start()
    spread[...] = spread_matrix(fb, n_t)
    target = lax.broadcasted_iota(jnp.int32, (tok, fb * n_t), 1) % n_t
    for b in range(n_blocks):
        cols = pl.ds(b * fb, fb)
        lat = ids[:, cols]
        chosen_b = chosen[...]
        hit = jnp.zeros((tok, fb), jnp.bool_)
        for k in range(chosen_b.shape[1]):
            hit = hit | (chosen_b[:, k:k + 1] == lat)
        on = hit.astype(F32)
        active[:, cols] = on
        pre = jnp.dot(feat[...], enc[:, cols], preferred_element_type=F32)
        code = (pre * on).astype(BF)
        codes[:, cols] = code
        rep = jnp.dot(code, spread[...], preferred_element_type=F32)
        for t in range(n_t):
            lhs[t * tok:(t + 1) * tok, :] = jnp.where(target == t, rep, 0.0).astype(BF)
        for cp in load_copies(dec, xin, sem, b, fb):
            cp.wait()

        @pl.loop(0, width // (128 * GROUP))
        def _(g):
            at = pl.ds(pl.multiple_of(g * 128 * GROUP, 128 * GROUP), 128 * GROUP)
            out = jnp.dot(lhs[...], wide(xin, g * GROUP, GROUP, b, fb),
                          preferred_element_type=F32)
            if b > 0:
                out = out + acc[:, at]
            if b < n_blocks - 1:
                acc[:, at] = out
            else:
                part[:, :, at] = out.astype(BF).reshape(n_t, tok, 128 * GROUP)


def decode(features, chosen, ids, enc, dec):
    lat_dev, n_t, width = dec.shape
    tok = features.shape[0]
    fb = 256
    n_blocks = lat_dev // fb
    vm = pl.BlockSpec(memory_space=pltpu.VMEM)
    return pl.pallas_call(
        functools.partial(decode_kernel, fb, n_blocks),
        out_shape=(jax.ShapeDtypeStruct((n_t, tok, width), BF),
                   jax.ShapeDtypeStruct((tok, lat_dev), BF),
                   jax.ShapeDtypeStruct((tok, lat_dev), F32)),
        in_specs=[vm, vm, vm, vm, pl.BlockSpec(memory_space=pl.ANY)],
        out_specs=(vm, vm, vm),
        scratch_shapes=[
            pltpu.VMEM((width // 128, lat_dev, n_t, 128), BF),
            pltpu.VMEM((n_t * tok, width), F32),
            pltpu.VMEM((n_t * tok, fb * n_t), BF),
            pltpu.VMEM((fb, fb * n_t), BF),
            pltpu.SemaphoreType.DMA((n_blocks, width // 128)),
        ],
        compiler_params=pltpu.CompilerParams(vmem_limit_bytes=52 * 2**20),
        cost_estimate=pl.CostEstimate(
            flops=10 * 10**9, bytes_accessed=2**24 + 2**22, transcendentals=0),
    )(features, chosen, ids, enc, dec)


def grad_kernel(fb, n_blocks, feat, codes, active, err, dec, grad_enc, grad_dec,
                xin, yout, gsum, lhs, spread, ebuf, sem, osem, esem):
    tok = feat.shape[0]
    rows_all, width = err.shape
    n_t = rows_all // tok
    for b in range(n_blocks):
        for cp in load_copies(dec, xin, sem, b, fb):
            cp.start()
    spread[...] = spread_matrix(fb, n_t)
    row_t = lax.broadcasted_iota(jnp.int32, (fb * n_t, tok), 0) % n_t
    col_t = lax.broadcasted_iota(jnp.int32, (tok, fb * n_t), 1) % n_t
    nt = (((1,), (1,)), ((), ()))
    cw = 128 * GROUP
    outs = []
    for b in range(n_blocks):
        cols = pl.ds(b * fb, fb)
        rep = lax.dot_general(spread[...], codes[:, cols], (((0,), (1,)), ((), ())),
                              preferred_element_type=F32)
        for t in range(n_t):
            lhs[:, t * tok:(t + 1) * tok] = jnp.where(row_t == t, rep, 0.0).astype(BF)

        @pl.loop(0, width // cw)
        def _(g):
            at = pl.ds(pl.multiple_of(g * cw, cw), cw)
            out = jnp.dot(lhs[...], err[:, at], preferred_element_type=F32).astype(BF)
            for j in range(GROUP):
                yout.at[g * GROUP + j, cols].reshape(fb * n_t, 128)[...] = (
                    out[:, j * 128:(j + 1) * 128])

        for j in range(width // 128):
            cp = pltpu.make_async_copy(yout.at[j, cols],
                                       grad_dec.at[cols, :, pl.ds(j * 128, 128)],
                                       osem.at[b, j])
            cp.start()
            outs.append(cp)
        for cp in load_copies(dec, xin, sem, b, fb):
            cp.wait()
        gsum[...] = jnp.zeros_like(gsum)

        @pl.loop(0, width // cw)
        def _(g):
            at = pl.ds(pl.multiple_of(g * cw, cw), cw)
            gsum[...] += lax.dot_general(err[:, at], wide(xin, g * GROUP, GROUP, b, fb), nt,
                                         preferred_element_type=F32)

        own = jnp.zeros((tok, fb * n_t), F32)
        for t in range(n_t):
            own = jnp.where(col_t == t, gsum[t * tok:(t + 1) * tok, :], own)
        high = own.astype(BF)
        low = (own - high.astype(F32)).astype(BF)
        code_grad = (lax.dot_general(high, spread[...], nt, preferred_element_type=F32)
                     + lax.dot_general(low, spread[...], nt, preferred_element_type=F32))
        pre_grad = (code_grad * active[:, cols]).astype(BF)
        ebuf[:, cols] = lax.dot_general(
            feat[...], pre_grad, (((0,), (0,)), ((), ())), preferred_element_type=F32
        ).astype(BF)
        cp = pltpu.make_async_copy(ebuf.at[:, cols], grad_enc.at[:, cols], esem.at[b])
        cp.start()
        outs.append(cp)
    for cp in outs:
        cp.wait()


def grads(features, codes, active, err, dec):
    lat_dev, n_t, width = dec.shape
    tok, d_in = features.shape
    fb = 256
    n_blocks = lat_dev // fb
    vm = pl.BlockSpec(memory_space=pltpu.VMEM)
    hbm = pl.BlockSpec(memory_space=pl.ANY)
    tiles = pltpu.VMEM((width // 128, lat_dev, n_t, 128), BF)
    return pl.pallas_call(
        functools.partial(grad_kernel, fb, n_blocks),
        out_shape=(jax.ShapeDtypeStruct((d_in, lat_dev), BF),
                   jax.ShapeDtypeStruct((lat_dev, n_t, width), BF)),
        in_specs=[vm, vm, vm, vm, hbm],
        out_specs=(hbm, hbm),
        scratch_shapes=[
            tiles, tiles,
            pltpu.VMEM((n_t * tok, fb * n_t), F32),
            pltpu.VMEM((fb * n_t, n_t * tok), BF),
            pltpu.VMEM((fb, fb * n_t), BF),
            pltpu.VMEM((d_in, lat_dev), BF),
            pltpu.SemaphoreType.DMA((n_blocks, width // 128)),
            pltpu.SemaphoreType.DMA((n_blocks, width // 128)),
            pltpu.SemaphoreType.DMA((n_blocks,)),
        ],
        compiler_params=pltpu.CompilerParams(vmem_limit_bytes=58 * 2**20),
        cost_estimate=pl.CostEstimate(
            flops=18 * 10**9, bytes_accessed=2**25 + 2**22, transcendentals=0),
    )(features, codes, active, err, dec)


def per_device(inputs, targets, top_index, enc_weight, dec_weight):
    n_layer = lax.axis_size("layer")
    n_lat = lax.axis_size("lat")
    layer_count = inputs.shape[0]
    tok_count = inputs.shape[1]
    lat_dev = enc_weight.shape[1]
    per_layer = n_layer // layer_count
    layer_id = lax.axis_index("layer") // per_layer
    lat_first = (lax.axis_index("layer") % per_layer * n_lat + lax.axis_index("lat")) * lat_dev
    tuned = (per_layer == 2 and layer_count == 4 and lat_dev % 256 == 0
             and targets.shape[0] * 2 * n_lat == tok_count and targets.shape[0] % 16 == 0
             and inputs.shape[2] % 256 == 0 and dec_weight.shape[2] % 512 == 0)
    if tuned:
        features = gather_features(inputs)
        chosen = lax.dynamic_index_in_dim(top_index, layer_id, 0, keepdims=False)
        ids = (lat_first + jnp.arange(lat_dev, dtype=jnp.int32))[None, :]
        part, codes, active = decode(features, chosen, ids, enc_weight, dec_weight)
        errors, err_used = exchange(part, targets)
        grad_enc, grad_dec = grads(
            features, codes, active, err_used.reshape(-1, err_used.shape[2]), dec_weight)
        return (errors, grad_enc, grad_dec)
    own_part = lax.dynamic_index_in_dim(inputs, layer_id, 0, keepdims=False)
    features = lax.all_gather(own_part, "lat", axis=1, tiled=True)
    preact = jnp.dot(features, enc_weight, preferred_element_type=jnp.float32)
    chosen = lax.dynamic_index_in_dim(top_index, layer_id, 0, keepdims=False)
    lat_ids = lat_first + jnp.arange(lat_dev, dtype=jnp.int32)
    active = jnp.any(chosen[:, :, None] == lat_ids[None, None, :], axis=1).astype(jnp.float32)
    code_vals = (preact * active).astype(jnp.bfloat16)
    reach_mask = (jnp.arange(layer_count, dtype=jnp.int32) >= layer_id).astype(jnp.float32)
    width = dec_weight.shape[2]
    row_count = targets.shape[0] * lax.axis_size(("layer", "lat"))
    result = jnp.einsum("nf,ftd->tnd", code_vals, dec_weight, preferred_element_type=jnp.float32)
    result = result * reach_mask[:, None, None]
    decoded = lax.psum_scatter(
        result.reshape(row_count, width), ("layer", "lat"), scatter_dimension=0, tiled=True
    )
    errors = decoded - targets.astype(jnp.float32)
    err_b = errors.astype(jnp.bfloat16)
    all_err = lax.all_gather(err_b, ("layer", "lat"), axis=0, tiled=True)
    err_used = (
        all_err.reshape(layer_count, tok_count, width)
        * reach_mask.astype(jnp.bfloat16)[:, None, None]
    )
    code_grad = jnp.einsum("lnd,fld->nf", err_used, dec_weight, preferred_element_type=jnp.float32)
    pre_grad = (code_grad * active).astype(jnp.bfloat16)
    grad_enc = lax.dot_general(
        features, pre_grad, (((0,), (0,)), ((), ())), preferred_element_type=jnp.float32
    ).astype(jnp.bfloat16)
    grad_dec = jnp.einsum(
        "nf,lnd->fld", code_vals, err_used, preferred_element_type=jnp.float32
    ).astype(jnp.bfloat16)
    return (errors, grad_enc, grad_dec)


def solution(mesh):
    in_specs = (
        P(None, None, "lat"),
        P(("layer", "lat"), None),
        P(),
        P(None, ("layer", "lat")),
        P(("layer", "lat"), None, None),
    )
    out_specs = (
        P(("layer", "lat"), None),
        P(None, ("layer", "lat")),
        P(("layer", "lat"), None, None),
    )
    return jax.shard_map(
        per_device, mesh=mesh, in_specs=in_specs, out_specs=out_specs, check_vma=False
    )
```

```python
import functools

import jax
import jax.numpy as jnp
from jax import lax
from jax.experimental import pallas as pl
from jax.experimental.pallas import tpu as pltpu
from jax.sharding import PartitionSpec as P

BF = jnp.bfloat16
F32 = jnp.float32


def spread_matrix(fb, n_t):
    f = lax.broadcasted_iota(jnp.int32, (fb, fb * n_t), 0)
    q = lax.broadcasted_iota(jnp.int32, (fb, fb * n_t), 1)
    return ((q >= f * n_t) & (q < (f + 1) * n_t)).astype(F32).astype(BF)


def load_copies(dec, xin, sem, block, fb):
    rows = pl.ds(block * fb, fb)
    return [pltpu.make_async_copy(dec.at[rows, :, pl.ds(j * 128, 128)],
                                  xin.at[j, rows], sem.at[block, j])
            for j in range(xin.shape[0])]


def wide(ref, first, count, block, fb):
    n_t = ref.shape[2]
    parts = [ref.at[first + j, pl.ds(block * fb, fb)].reshape(fb * n_t, 128)[...]
             for j in range(count)]
    return jnp.concatenate(parts, axis=1)


GROUP = 4


def forward_kernel(n_t, n_lat, own, targets, chosen, ids, enc, dec,
                   errors, all_err, feat, codes, active,
                   xin, lhs, spread, acc, part, sib_rx, q, xy_rx, zs, z_rx, load_sem,
                   s1, r1, s2, r2, s3, r3, s4, r4, s5, r5, s6, r6, s7, r7, s8, r8):
    row = lax.axis_index("layer")
    z = lax.axis_index("lat")
    s = row // 2
    c = row % 2
    width = part.shape[2]
    half = part.shape[1] // 2
    rows = half // n_lat
    cw = 128 * GROUP
    chunks = width // cw
    fb = spread.shape[0]
    n_blocks = codes.shape[1] // fb
    cut = own.shape[2]
    piece = cut // 2
    sibling = (s * 2 + 1 - c, z)
    mine = pl.ds(pl.multiple_of(c * half, half), half)
    other = pl.ds(pl.multiple_of((1 - c) * half, half), half)

    def col(t):
        return (2 * t + c, z)

    def lat(zz):
        return (row, zz)

    def cols(ch):
        return pl.ds(ch * cw, cw)

    def rblock(zz):
        return pl.ds(pl.multiple_of(zz * rows, rows), rows)

    def eblock(zz):
        return pl.ds(pl.multiple_of(c * half + zz * rows, rows), rows)

    def copy(src, dst, ssem, rsem, dev):
        return pltpu.make_async_remote_copy(
            src_ref=src, dst_ref=dst, send_sem=ssem, recv_sem=rsem,
            device_id=dev, device_id_type=pl.DeviceIdType.MESH)

    loads = [pltpu.make_async_copy(dec.at[:, :, pl.ds(j * 128, 128)], xin.at[j], load_sem.at[j])
             for j in range(width // 128)]
    for cp in loads:
        cp.start()

    barrier = pltpu.get_barrier_semaphore()
    pl.semaphore_signal(barrier, inc=1, device_id=sibling, device_id_type=pl.DeviceIdType.MESH)
    for t in range(n_t):
        @pl.when(t != s)
        def _():
            pl.semaphore_signal(barrier, inc=1, device_id=col(t), device_id_type=pl.DeviceIdType.MESH)
    for zz in range(n_lat):
        @pl.when(zz != z)
        def _():
            pl.semaphore_signal(barrier, inc=1, device_id=lat(zz), device_id_type=pl.DeviceIdType.MESH)
    pl.semaphore_wait(barrier, n_t + n_lat - 1)

    def pair(ch, t):
        return copy(part.at[t, other, cols(ch)], sib_rx.at[t, :, cols(ch)],
                    s1.at[ch, t], r1.at[ch, t], sibling)

    def to_target(ch, t):
        return copy(q.at[t, :, cols(ch)], xy_rx.at[s, :, cols(ch)],
                    s2.at[ch, t], r2.at[ch, s], col(t))

    def from_source(ch, ss):
        return copy(q.at[ss, :, cols(ch)], xy_rx.at[ss, :, cols(ch)],
                    s2.at[ch, ss], r2.at[ch, ss], col(ss))

    def to_lat(ch, zz):
        return copy(zs.at[rblock(zz), cols(ch)], z_rx.at[z, :, cols(ch)],
                    s3.at[ch, zz], r3.at[ch, z], lat(zz))

    def from_lat(ch, zz):
        return copy(zs.at[rblock(zz), cols(ch)], z_rx.at[zz, :, cols(ch)],
                    s3.at[ch, zz], r3.at[ch, zz], lat(zz))

    def err_to_lat(ch, zz):
        return copy(all_err.at[s, eblock(z), cols(ch)], all_err.at[s, eblock(z), cols(ch)],
                    s4.at[ch, zz], r4.at[ch, z], lat(zz))

    def err_from_lat(ch, zz):
        return copy(all_err.at[s, eblock(zz), cols(ch)], all_err.at[s, eblock(zz), cols(ch)],
                    s4.at[ch, zz], r4.at[ch, zz], lat(zz))

    def err_to_source(ch, ss):
        return copy(all_err.at[s, mine, cols(ch)], all_err.at[s, mine, cols(ch)],
                    s5.at[ch, ss], r5.at[ch, s], col(ss))

    def err_from_target(ch, t):
        return copy(all_err.at[t, mine, cols(ch)], all_err.at[t, mine, cols(ch)],
                    s5.at[ch, t], r5.at[ch, t], col(t))

    def err_pair(ch, t):
        return copy(all_err.at[t, mine, cols(ch)], all_err.at[t, mine, cols(ch)],
                    s6.at[ch, t], r6.at[ch, t], sibling)

    def err_pair_in(ch, t):
        return copy(all_err.at[t, other, cols(ch)], all_err.at[t, other, cols(ch)],
                    s6.at[ch, t], r6.at[ch, t], sibling)

    def fcols(zz, cc):
        return pl.ds(pl.multiple_of(zz * cut + cc * piece, piece), piece)

    def send(zz):
        return copy(own.at[s, :, pl.ds(pl.multiple_of(c * piece, piece), piece)],
                    feat.at[:, fcols(z, c)], s7.at[zz], r7.at[z], lat(zz))

    def arrive(zz):
        return copy(feat.at[:, fcols(zz, c)], feat.at[:, fcols(zz, c)],
                    s7.at[zz], r7.at[zz], lat(zz))

    def forward(zz, cc):
        return copy(feat.at[:, fcols(zz, cc)], feat.at[:, fcols(zz, cc)],
                    s8.at[zz], r8.at[zz], sibling)

    for zz in range(n_lat):
        @pl.when(zz != z)
        def _():
            send(zz).start()
    feat[:, pl.ds(pl.multiple_of(z * cut, cut), cut)] = own[s]
    for t in range(n_t):
        @pl.when(t < s)
        def _():
            all_err[t] = jnp.zeros((2 * half, width), BF)
    tok = 2 * half
    spread[...] = spread_matrix(fb, n_t)
    target = lax.broadcasted_iota(jnp.int32, (tok, fb * n_t), 1) % n_t

    @pl.loop(0, n_blocks)
    def _(b):
        at = pl.ds(pl.multiple_of(b * fb, fb), fb)
        lats = ids[:, at]
        picks = chosen[...]
        hit = jnp.zeros((tok, fb), jnp.bool_)
        for k in range(picks.shape[1]):
            hit = hit | (picks[:, k:k + 1] == lats)
        active[:, at] = hit.astype(F32)

    for zz in range(n_lat):
        @pl.when(zz != z)
        def _():
            arrive(zz).wait_recv()
            forward(zz, c).start()
    for zz in range(n_lat):
        @pl.when(zz != z)
        def _():
            forward(zz, 1 - c).wait_recv()

    @pl.loop(0, n_blocks)
    def _(b):
        at = pl.ds(pl.multiple_of(b * fb, fb), fb)
        wide_at = pl.ds(pl.multiple_of(b * fb * n_t, fb * n_t), fb * n_t)
        pre = jnp.dot(feat[...], enc[:, at], preferred_element_type=F32)
        code = (pre * active[:, at]).astype(BF)
        codes[:, at] = code
        rep = jnp.dot(code, spread[...], preferred_element_type=F32)
        for t in range(n_t):
            lhs[t * tok:(t + 1) * tok, wide_at] = jnp.where(target == t, rep, 0.0).astype(BF)

    def decode_chunk(ch):
        for j in range(GROUP):
            loads[ch * GROUP + j].wait()
        acc[...] = jnp.zeros_like(acc)

        @pl.loop(0, n_blocks)
        def _(b):
            wide_at = pl.ds(pl.multiple_of(b * fb * n_t, fb * n_t), fb * n_t)
            acc[...] += jnp.dot(lhs[:, wide_at], wide(xin, ch * GROUP, GROUP, b, fb),
                                preferred_element_type=F32)

        part[:, :, cols(ch)] = acc[...].astype(BF).reshape(n_t, tok, cw)
        for t in reversed(range(n_t)):
            @pl.when(t >= s)
            def _():
                pair(ch, t).start()

    def add_pair(ch):
        for t in reversed(range(n_t)):
            @pl.when(t >= s)
            def _():
                pair(ch, t).wait_recv()

            @pl.when(t > s)
            def _():
                q[t, :, cols(ch)] = (part[t, mine, cols(ch)].astype(F32)
                                     + sib_rx[t, :, cols(ch)].astype(F32)).astype(BF)
                to_target(ch, t).start()

    def add_sources(ch):
        for ss in range(n_t):
            @pl.when(ss == s)
            def _():
                total = (part[ss, mine, cols(ch)].astype(F32)
                         + sib_rx[ss, :, cols(ch)].astype(F32))
                for src in range(ss):
                    from_source(ch, src).wait_recv()
                    total = total + xy_rx[src, :, cols(ch)].astype(F32)
                zs[:, cols(ch)] = total.astype(BF)
        for zz in range(n_lat):
            @pl.when(zz != z)
            def _():
                to_lat(ch, zz).start()

    def finish(ch):
        z_rx[z, :, cols(ch)] = zs[rblock(z), cols(ch)]
        for zz in range(n_lat):
            @pl.when(zz != z)
            def _():
                from_lat(ch, zz).wait_recv()
        total = z_rx[0, :, cols(ch)].astype(F32)
        for zz in range(1, n_lat):
            total = total + z_rx[zz, :, cols(ch)].astype(F32)
        err = total - targets[:, cols(ch)].astype(F32)
        errors[:, cols(ch)] = err
        all_err[s, eblock(z), cols(ch)] = err.astype(BF)
        for zz in range(n_lat):
            @pl.when(zz != z)
            def _():
                err_to_lat(ch, zz).start()

    def spread_err(ch):
        for zz in range(n_lat):
            @pl.when(zz != z)
            def _():
                err_from_lat(ch, zz).wait_recv()
        for ss in range(n_t):
            @pl.when(ss < s)
            def _():
                err_to_source(ch, ss).start()
        err_pair(ch, s).start()

    def relay_err(ch):
        for t in range(n_t):
            @pl.when(t > s)
            def _():
                err_from_target(ch, t).wait_recv()
                err_pair(ch, t).start()

    def drain(ch):
        for t in range(n_t):
            @pl.when(t >= s)
            def _():
                err_pair_in(ch, t).wait_recv()
                err_pair(ch, t).wait_send()
                pair(ch, t).wait_send()

            @pl.when(t > s)
            def _():
                to_target(ch, t).wait_send()

            @pl.when(t < s)
            def _():
                err_to_source(ch, t).wait_send()
        for zz in range(n_lat):
            @pl.when(zz != z)
            def _():
                to_lat(ch, zz).wait_send()
                err_to_lat(ch, zz).wait_send()

    stages = (decode_chunk, add_pair, add_sources, finish, spread_err, relay_err)
    for step in range(chunks + len(stages) - 1):
        for lag, stage in enumerate(stages):
            if 0 <= step - lag < chunks:
                stage(step - lag)
    for ch in range(chunks):
        drain(ch)
    for zz in range(n_lat):
        @pl.when(zz != z)
        def _():
            forward(zz, c).wait_send()
            send(zz).wait_send()


def forward_pass(inputs, targets, chosen, ids, enc, dec):
    n_lat = lax.axis_size("lat")
    lat_dev, n_t, width = dec.shape
    tok = inputs.shape[1]
    half = tok // 2
    rows = half // n_lat
    fb = 256
    chunks = width // (128 * GROUP)
    vm = pl.BlockSpec(memory_space=pltpu.VMEM)
    dma = pltpu.SemaphoreType.DMA
    sems = []
    for n in (n_t, n_t, n_lat, n_lat, n_t, n_t):
        sems += [dma((chunks, n)), dma((chunks, n))]
    return pl.pallas_call(
        functools.partial(forward_kernel, n_t, n_lat),
        out_shape=(jax.ShapeDtypeStruct((rows, width), F32),
                   jax.ShapeDtypeStruct((n_t, tok, width), BF),
                   jax.ShapeDtypeStruct((tok, enc.shape[0]), BF),
                   jax.ShapeDtypeStruct((tok, lat_dev), BF),
                   jax.ShapeDtypeStruct((tok, lat_dev), F32)),
        in_specs=[vm, vm, vm, vm, vm, pl.BlockSpec(memory_space=pl.ANY)],
        out_specs=(vm, vm, vm, vm, vm),
        scratch_shapes=[
            pltpu.VMEM((width // 128, lat_dev, n_t, 128), BF),
            pltpu.VMEM((n_t * tok, lat_dev * n_t), BF),
            pltpu.VMEM((fb, fb * n_t), BF),
            pltpu.VMEM((n_t * tok, 128 * GROUP), F32),
            pltpu.VMEM((n_t, tok, width), BF),
            pltpu.VMEM((n_t, half, width), BF),
            pltpu.VMEM((n_t, half, width), BF),
            pltpu.VMEM((n_t, half, width), BF),
            pltpu.VMEM((half, width), BF),
            pltpu.VMEM((n_lat, rows, width), BF),
            dma((width // 128,)),
        ] + sems + [dma((n_lat,))] * 4,
        compiler_params=pltpu.CompilerParams(
            collective_id=0, has_side_effects=True, vmem_limit_bytes=56 * 2**20),
        cost_estimate=pl.CostEstimate(
            flops=10 * 10**9, bytes_accessed=2**24 + 2**22, transcendentals=0),
    )(inputs, targets, chosen, ids, enc, dec)


def grad_kernel(fb, n_blocks, feat, codes, active, err, dec, grad_enc, grad_dec,
                xin, yout, gsum, lhs, spread, ebuf, sem, osem, esem):
    tok = feat.shape[0]
    rows_all, width = err.shape
    n_t = rows_all // tok
    for b in range(n_blocks):
        for cp in load_copies(dec, xin, sem, b, fb):
            cp.start()
    spread[...] = spread_matrix(fb, n_t)
    row_t = lax.broadcasted_iota(jnp.int32, (fb * n_t, tok), 0) % n_t
    col_t = lax.broadcasted_iota(jnp.int32, (tok, fb * n_t), 1) % n_t
    nt = (((1,), (1,)), ((), ()))
    cw = 128 * GROUP
    outs = []
    for b in range(n_blocks):
        cols = pl.ds(b * fb, fb)
        rep = lax.dot_general(spread[...], codes[:, cols], (((0,), (1,)), ((), ())),
                              preferred_element_type=F32)
        for t in range(n_t):
            lhs[:, t * tok:(t + 1) * tok] = jnp.where(row_t == t, rep, 0.0).astype(BF)

        @pl.loop(0, width // cw)
        def _(g):
            at = pl.ds(pl.multiple_of(g * cw, cw), cw)
            out = jnp.dot(lhs[...], err[:, at], preferred_element_type=F32).astype(BF)
            for j in range(GROUP):
                yout.at[g * GROUP + j, cols].reshape(fb * n_t, 128)[...] = (
                    out[:, j * 128:(j + 1) * 128])

        for j in range(width // 128):
            cp = pltpu.make_async_copy(yout.at[j, cols],
                                       grad_dec.at[cols, :, pl.ds(j * 128, 128)],
                                       osem.at[b, j])
            cp.start()
            outs.append(cp)
        for cp in load_copies(dec, xin, sem, b, fb):
            cp.wait()
        gsum[...] = jnp.zeros_like(gsum)

        @pl.loop(0, width // cw)
        def _(g):
            at = pl.ds(pl.multiple_of(g * cw, cw), cw)
            gsum[...] += lax.dot_general(err[:, at], wide(xin, g * GROUP, GROUP, b, fb), nt,
                                         preferred_element_type=F32)

        own = jnp.zeros((tok, fb * n_t), F32)
        for t in range(n_t):
            own = jnp.where(col_t == t, gsum[t * tok:(t + 1) * tok, :], own)
        high = own.astype(BF)
        low = (own - high.astype(F32)).astype(BF)
        code_grad = (lax.dot_general(high, spread[...], nt, preferred_element_type=F32)
                     + lax.dot_general(low, spread[...], nt, preferred_element_type=F32))
        pre_grad = (code_grad * active[:, cols]).astype(BF)
        ebuf[:, cols] = lax.dot_general(
            feat[...], pre_grad, (((0,), (0,)), ((), ())), preferred_element_type=F32
        ).astype(BF)
        cp = pltpu.make_async_copy(ebuf.at[:, cols], grad_enc.at[:, cols], esem.at[b])
        cp.start()
        outs.append(cp)
    for cp in outs:
        cp.wait()


def grads(features, codes, active, err, dec):
    lat_dev, n_t, width = dec.shape
    tok, d_in = features.shape
    fb = 256
    n_blocks = lat_dev // fb
    vm = pl.BlockSpec(memory_space=pltpu.VMEM)
    hbm = pl.BlockSpec(memory_space=pl.ANY)
    tiles = pltpu.VMEM((width // 128, lat_dev, n_t, 128), BF)
    return pl.pallas_call(
        functools.partial(grad_kernel, fb, n_blocks),
        out_shape=(jax.ShapeDtypeStruct((d_in, lat_dev), BF),
                   jax.ShapeDtypeStruct((lat_dev, n_t, width), BF)),
        in_specs=[vm, vm, vm, vm, hbm],
        out_specs=(hbm, hbm),
        scratch_shapes=[
            tiles, tiles,
            pltpu.VMEM((n_t * tok, fb * n_t), F32),
            pltpu.VMEM((fb * n_t, n_t * tok), BF),
            pltpu.VMEM((fb, fb * n_t), BF),
            pltpu.VMEM((d_in, lat_dev), BF),
            pltpu.SemaphoreType.DMA((n_blocks, width // 128)),
            pltpu.SemaphoreType.DMA((n_blocks, width // 128)),
            pltpu.SemaphoreType.DMA((n_blocks,)),
        ],
        compiler_params=pltpu.CompilerParams(vmem_limit_bytes=58 * 2**20),
        cost_estimate=pl.CostEstimate(
            flops=18 * 10**9, bytes_accessed=2**25 + 2**22, transcendentals=0),
    )(features, codes, active, err, dec)


def per_device(inputs, targets, top_index, enc_weight, dec_weight):
    n_layer = lax.axis_size("layer")
    n_lat = lax.axis_size("lat")
    layer_count = inputs.shape[0]
    tok_count = inputs.shape[1]
    lat_dev = enc_weight.shape[1]
    per_layer = n_layer // layer_count
    layer_id = lax.axis_index("layer") // per_layer
    lat_first = (lax.axis_index("layer") % per_layer * n_lat + lax.axis_index("lat")) * lat_dev
    tuned = (per_layer == 2 and layer_count == 4 and lat_dev % 256 == 0
             and targets.shape[0] * 2 * n_lat == tok_count and targets.shape[0] % 16 == 0
             and inputs.shape[2] % 256 == 0 and dec_weight.shape[2] % 512 == 0)
    if tuned:
        chosen = lax.dynamic_index_in_dim(top_index, layer_id, 0, keepdims=False)
        ids = (lat_first + jnp.arange(lat_dev, dtype=jnp.int32))[None, :]
        errors, err_used, features, codes, active = forward_pass(
            inputs, targets, chosen, ids, enc_weight, dec_weight)
        grad_enc, grad_dec = grads(
            features, codes, active, err_used.reshape(-1, err_used.shape[2]), dec_weight)
        return (errors, grad_enc, grad_dec)
    own_part = lax.dynamic_index_in_dim(inputs, layer_id, 0, keepdims=False)
    features = lax.all_gather(own_part, "lat", axis=1, tiled=True)
    preact = jnp.dot(features, enc_weight, preferred_element_type=jnp.float32)
    chosen = lax.dynamic_index_in_dim(top_index, layer_id, 0, keepdims=False)
    lat_ids = lat_first + jnp.arange(lat_dev, dtype=jnp.int32)
    active = jnp.any(chosen[:, :, None] == lat_ids[None, None, :], axis=1).astype(jnp.float32)
    code_vals = (preact * active).astype(jnp.bfloat16)
    reach_mask = (jnp.arange(layer_count, dtype=jnp.int32) >= layer_id).astype(jnp.float32)
    width = dec_weight.shape[2]
    row_count = targets.shape[0] * lax.axis_size(("layer", "lat"))
    result = jnp.einsum("nf,ftd->tnd", code_vals, dec_weight, preferred_element_type=jnp.float32)
    result = result * reach_mask[:, None, None]
    decoded = lax.psum_scatter(
        result.reshape(row_count, width), ("layer", "lat"), scatter_dimension=0, tiled=True
    )
    errors = decoded - targets.astype(jnp.float32)
    err_b = errors.astype(jnp.bfloat16)
    all_err = lax.all_gather(err_b, ("layer", "lat"), axis=0, tiled=True)
    err_used = (
        all_err.reshape(layer_count, tok_count, width)
        * reach_mask.astype(jnp.bfloat16)[:, None, None]
    )
    code_grad = jnp.einsum("lnd,fld->nf", err_used, dec_weight, preferred_element_type=jnp.float32)
    pre_grad = (code_grad * active).astype(jnp.bfloat16)
    grad_enc = lax.dot_general(
        features, pre_grad, (((0,), (0,)), ((), ())), preferred_element_type=jnp.float32
    ).astype(jnp.bfloat16)
    grad_dec = jnp.einsum(
        "nf,lnd->fld", code_vals, err_used, preferred_element_type=jnp.float32
    ).astype(jnp.bfloat16)
    return (errors, grad_enc, grad_dec)


def solution(mesh):
    in_specs = (
        P(None, None, "lat"),
        P(("layer", "lat"), None),
        P(),
        P(None, ("layer", "lat")),
        P(("layer", "lat"), None, None),
    )
    out_specs = (
        P(("layer", "lat"), None),
        P(None, ("layer", "lat")),
        P(("layer", "lat"), None, None),
    )
    return jax.shard_map(
        per_device, mesh=mesh, in_specs=in_specs, out_specs=out_specs, check_vma=False
    )
```

```python
import functools

import jax
import jax.numpy as jnp
from jax import lax
from jax.experimental import pallas as pl
from jax.experimental.pallas import tpu as pltpu
from jax.sharding import PartitionSpec as P

BF = jnp.bfloat16
F32 = jnp.float32


def spread_matrix(fb, n_t):
    f = lax.broadcasted_iota(jnp.int32, (fb, fb * n_t), 0)
    q = lax.broadcasted_iota(jnp.int32, (fb, fb * n_t), 1)
    return ((q >= f * n_t) & (q < (f + 1) * n_t)).astype(F32).astype(BF)


def load_copies(dec, xin, sem, block, fb):
    rows = pl.ds(block * fb, fb)
    return [pltpu.make_async_copy(dec.at[rows, :, pl.ds(j * 128, 128)],
                                  xin.at[j, rows], sem.at[block, j])
            for j in range(xin.shape[0])]


def wide(ref, first, count, block, fb):
    n_t = ref.shape[2]
    parts = [ref.at[first + j, pl.ds(block * fb, fb)].reshape(fb * n_t, 128)[...]
             for j in range(count)]
    return jnp.concatenate(parts, axis=1)


GROUP = 4
CHUNK = 2


def forward_kernel(n_t, n_lat, own, targets, chosen, ids, enc, dec,
                   errors, all_err, feat, codes, active,
                   xin, lhs, spread, acc, part, sib_rx, q, xy_rx, zs, z_rx, load_sem,
                   s1, r1, s2, r2, s3, r3, s4, r4, s5, r5, s6, r6, s7, r7, s8, r8):
    row = lax.axis_index("layer")
    z = lax.axis_index("lat")
    s = row // 2
    c = row % 2
    width = part.shape[2]
    half = part.shape[1] // 2
    rows = half // n_lat
    cw = 128 * CHUNK
    chunks = width // cw
    fb = spread.shape[0]
    n_blocks = codes.shape[1] // fb
    cut = own.shape[2]
    piece = cut // 2
    sibling = (s * 2 + 1 - c, z)
    mine = pl.ds(pl.multiple_of(c * half, half), half)
    other = pl.ds(pl.multiple_of((1 - c) * half, half), half)

    def col(t):
        return (2 * t + c, z)

    def lat(zz):
        return (row, zz)

    def cols(ch):
        return pl.ds(ch * cw, cw)

    def rblock(zz):
        return pl.ds(pl.multiple_of(zz * rows, rows), rows)

    def eblock(zz):
        return pl.ds(pl.multiple_of(c * half + zz * rows, rows), rows)

    def copy(src, dst, ssem, rsem, dev):
        return pltpu.make_async_remote_copy(
            src_ref=src, dst_ref=dst, send_sem=ssem, recv_sem=rsem,
            device_id=dev, device_id_type=pl.DeviceIdType.MESH)

    loads = [pltpu.make_async_copy(dec.at[:, :, pl.ds(j * 128, 128)], xin.at[j], load_sem.at[j])
             for j in range(width // 128)]
    for cp in loads:
        cp.start()

    barrier = pltpu.get_barrier_semaphore()
    pl.semaphore_signal(barrier, inc=1, device_id=sibling, device_id_type=pl.DeviceIdType.MESH)
    for t in range(n_t):
        @pl.when(t != s)
        def _():
            pl.semaphore_signal(barrier, inc=1, device_id=col(t), device_id_type=pl.DeviceIdType.MESH)
    for zz in range(n_lat):
        @pl.when(zz != z)
        def _():
            pl.semaphore_signal(barrier, inc=1, device_id=lat(zz), device_id_type=pl.DeviceIdType.MESH)
    pl.semaphore_wait(barrier, n_t + n_lat - 1)

    def pair(ch, t):
        return copy(part.at[t, other, cols(ch)], sib_rx.at[t, :, cols(ch)],
                    s1.at[ch, t], r1.at[ch, t], sibling)

    def to_target(ch, t):
        return copy(q.at[t, :, cols(ch)], xy_rx.at[s, :, cols(ch)],
                    s2.at[ch, t], r2.at[ch, s], col(t))

    def from_source(ch, ss):
        return copy(q.at[ss, :, cols(ch)], xy_rx.at[ss, :, cols(ch)],
                    s2.at[ch, ss], r2.at[ch, ss], col(ss))

    def to_lat(ch, zz):
        return copy(zs.at[rblock(zz), cols(ch)], z_rx.at[z, :, cols(ch)],
                    s3.at[ch, zz], r3.at[ch, z], lat(zz))

    def from_lat(ch, zz):
        return copy(zs.at[rblock(zz), cols(ch)], z_rx.at[zz, :, cols(ch)],
                    s3.at[ch, zz], r3.at[ch, zz], lat(zz))

    def err_to_lat(ch, zz):
        return copy(all_err.at[s, eblock(z), cols(ch)], all_err.at[s, eblock(z), cols(ch)],
                    s4.at[ch, zz], r4.at[ch, z], lat(zz))

    def err_from_lat(ch, zz):
        return copy(all_err.at[s, eblock(zz), cols(ch)], all_err.at[s, eblock(zz), cols(ch)],
                    s4.at[ch, zz], r4.at[ch, zz], lat(zz))

    def err_to_source(ch, ss):
        return copy(all_err.at[s, mine, cols(ch)], all_err.at[s, mine, cols(ch)],
                    s5.at[ch, ss], r5.at[ch, s], col(ss))

    def err_from_target(ch, t):
        return copy(all_err.at[t, mine, cols(ch)], all_err.at[t, mine, cols(ch)],
                    s5.at[ch, t], r5.at[ch, t], col(t))

    def err_pair(ch, t):
        return copy(all_err.at[t, mine, cols(ch)], all_err.at[t, mine, cols(ch)],
                    s6.at[ch, t], r6.at[ch, t], sibling)

    def err_pair_in(ch, t):
        return copy(all_err.at[t, other, cols(ch)], all_err.at[t, other, cols(ch)],
                    s6.at[ch, t], r6.at[ch, t], sibling)

    def fcols(zz, cc):
        return pl.ds(pl.multiple_of(zz * cut + cc * piece, piece), piece)

    def send(zz):
        return copy(own.at[s, :, pl.ds(pl.multiple_of(c * piece, piece), piece)],
                    feat.at[:, fcols(z, c)], s7.at[zz], r7.at[z], lat(zz))

    def arrive(zz):
        return copy(feat.at[:, fcols(zz, c)], feat.at[:, fcols(zz, c)],
                    s7.at[zz], r7.at[zz], lat(zz))

    def forward(zz, cc):
        return copy(feat.at[:, fcols(zz, cc)], feat.at[:, fcols(zz, cc)],
                    s8.at[zz], r8.at[zz], sibling)

    for zz in range(n_lat):
        @pl.when(zz != z)
        def _():
            send(zz).start()
    feat[:, pl.ds(pl.multiple_of(z * cut, cut), cut)] = own[s]
    for t in range(n_t):
        @pl.when(t < s)
        def _():
            all_err[t] = jnp.zeros((2 * half, width), BF)
    tok = 2 * half
    spread[...] = spread_matrix(fb, n_t)
    target = lax.broadcasted_iota(jnp.int32, (tok, fb * n_t), 1) % n_t

    @pl.loop(0, n_blocks)
    def _(b):
        at = pl.ds(pl.multiple_of(b * fb, fb), fb)
        lats = ids[:, at]
        picks = chosen[...]
        hit = jnp.zeros((tok, fb), jnp.bool_)
        for k in range(picks.shape[1]):
            hit = hit | (picks[:, k:k + 1] == lats)
        active[:, at] = hit.astype(F32)

    for zz in range(n_lat):
        @pl.when(zz != z)
        def _():
            arrive(zz).wait_recv()
            forward(zz, c).start()
    for zz in range(n_lat):
        @pl.when(zz != z)
        def _():
            forward(zz, 1 - c).wait_recv()

    @pl.loop(0, n_blocks)
    def _(b):
        at = pl.ds(pl.multiple_of(b * fb, fb), fb)
        wide_at = pl.ds(pl.multiple_of(b * fb * n_t, fb * n_t), fb * n_t)
        pre = jnp.dot(feat[...], enc[:, at], preferred_element_type=F32)
        code = (pre * active[:, at]).astype(BF)
        codes[:, at] = code
        rep = jnp.dot(code, spread[...], preferred_element_type=F32)
        for t in range(n_t):
            lhs[t * tok:(t + 1) * tok, wide_at] = jnp.where(target == t, rep, 0.0).astype(BF)

    def decode_chunk(ch):
        for j in range(CHUNK):
            loads[ch * CHUNK + j].wait()
        acc[...] = jnp.zeros_like(acc)

        @pl.loop(0, n_blocks)
        def _(b):
            wide_at = pl.ds(pl.multiple_of(b * fb * n_t, fb * n_t), fb * n_t)
            acc[...] += jnp.dot(lhs[:, wide_at], wide(xin, ch * CHUNK, CHUNK, b, fb),
                                preferred_element_type=F32)

        part[:, :, cols(ch)] = acc[...].astype(BF).reshape(n_t, tok, cw)
        for t in reversed(range(n_t)):
            @pl.when(t >= s)
            def _():
                pair(ch, t).start()

    def add_pair(ch):
        for t in reversed(range(n_t)):
            @pl.when(t >= s)
            def _():
                pair(ch, t).wait_recv()

            @pl.when(t > s)
            def _():
                q[t, :, cols(ch)] = (part[t, mine, cols(ch)].astype(F32)
                                     + sib_rx[t, :, cols(ch)].astype(F32)).astype(BF)
                to_target(ch, t).start()

    def add_sources(ch):
        for ss in range(n_t):
            @pl.when(ss == s)
            def _():
                total = (part[ss, mine, cols(ch)].astype(F32)
                         + sib_rx[ss, :, cols(ch)].astype(F32))
                for src in range(ss):
                    from_source(ch, src).wait_recv()
                    total = total + xy_rx[src, :, cols(ch)].astype(F32)
                zs[:, cols(ch)] = total.astype(BF)
        for zz in range(n_lat):
            @pl.when(zz != z)
            def _():
                to_lat(ch, zz).start()

    def finish(ch):
        z_rx[z, :, cols(ch)] = zs[rblock(z), cols(ch)]
        for zz in range(n_lat):
            @pl.when(zz != z)
            def _():
                from_lat(ch, zz).wait_recv()
        total = z_rx[0, :, cols(ch)].astype(F32)
        for zz in range(1, n_lat):
            total = total + z_rx[zz, :, cols(ch)].astype(F32)
        err = total - targets[:, cols(ch)].astype(F32)
        errors[:, cols(ch)] = err
        all_err[s, eblock(z), cols(ch)] = err.astype(BF)
        for zz in range(n_lat):
            @pl.when(zz != z)
            def _():
                err_to_lat(ch, zz).start()

    def spread_err(ch):
        for zz in range(n_lat):
            @pl.when(zz != z)
            def _():
                err_from_lat(ch, zz).wait_recv()
        for ss in range(n_t):
            @pl.when(ss < s)
            def _():
                err_to_source(ch, ss).start()
        err_pair(ch, s).start()

    def relay_err(ch):
        for t in range(n_t):
            @pl.when(t > s)
            def _():
                err_from_target(ch, t).wait_recv()
                err_pair(ch, t).start()

    def drain(ch):
        for t in range(n_t):
            @pl.when(t >= s)
            def _():
                err_pair_in(ch, t).wait_recv()
                err_pair(ch, t).wait_send()
                pair(ch, t).wait_send()

            @pl.when(t > s)
            def _():
                to_target(ch, t).wait_send()

            @pl.when(t < s)
            def _():
                err_to_source(ch, t).wait_send()
        for zz in range(n_lat):
            @pl.when(zz != z)
            def _():
                to_lat(ch, zz).wait_send()
                err_to_lat(ch, zz).wait_send()

    stages = (decode_chunk, add_pair, add_sources, finish, spread_err, relay_err)
    for step in range(chunks + len(stages) - 1):
        for lag, stage in enumerate(stages):
            if 0 <= step - lag < chunks:
                stage(step - lag)
    for ch in range(chunks):
        drain(ch)
    for zz in range(n_lat):
        @pl.when(zz != z)
        def _():
            forward(zz, c).wait_send()
            send(zz).wait_send()


def forward_pass(inputs, targets, chosen, ids, enc, dec):
    n_lat = lax.axis_size("lat")
    lat_dev, n_t, width = dec.shape
    tok = inputs.shape[1]
    half = tok // 2
    rows = half // n_lat
    fb = 256
    chunks = width // (128 * CHUNK)
    vm = pl.BlockSpec(memory_space=pltpu.VMEM)
    dma = pltpu.SemaphoreType.DMA
    sems = []
    for n in (n_t, n_t, n_lat, n_lat, n_t, n_t):
        sems += [dma((chunks, n)), dma((chunks, n))]
    return pl.pallas_call(
        functools.partial(forward_kernel, n_t, n_lat),
        out_shape=(jax.ShapeDtypeStruct((rows, width), F32),
                   jax.ShapeDtypeStruct((n_t, tok, width), BF),
                   jax.ShapeDtypeStruct((tok, enc.shape[0]), BF),
                   jax.ShapeDtypeStruct((tok, lat_dev), BF),
                   jax.ShapeDtypeStruct((tok, lat_dev), F32)),
        in_specs=[vm, vm, vm, vm, vm, pl.BlockSpec(memory_space=pl.ANY)],
        out_specs=(vm, vm, vm, vm, vm),
        scratch_shapes=[
            pltpu.VMEM((width // 128, lat_dev, n_t, 128), BF),
            pltpu.VMEM((n_t * tok, lat_dev * n_t), BF),
            pltpu.VMEM((fb, fb * n_t), BF),
            pltpu.VMEM((n_t * tok, 128 * CHUNK), F32),
            pltpu.VMEM((n_t, tok, width), BF),
            pltpu.VMEM((n_t, half, width), BF),
            pltpu.VMEM((n_t, half, width), BF),
            pltpu.VMEM((n_t, half, width), BF),
            pltpu.VMEM((half, width), BF),
            pltpu.VMEM((n_lat, rows, width), BF),
            dma((width // 128,)),
        ] + sems + [dma((n_lat,))] * 4,
        compiler_params=pltpu.CompilerParams(
            collective_id=0, has_side_effects=True, vmem_limit_bytes=56 * 2**20),
        cost_estimate=pl.CostEstimate(
            flops=10 * 10**9, bytes_accessed=2**24 + 2**22, transcendentals=0),
    )(inputs, targets, chosen, ids, enc, dec)


def grad_kernel(fb, n_blocks, feat, codes, active, err, dec, grad_enc, grad_dec,
                xin, yout, gsum, lhs, spread, ebuf, sem, osem, esem):
    tok = feat.shape[0]
    rows_all, width = err.shape
    n_t = rows_all // tok
    for b in range(n_blocks):
        for cp in load_copies(dec, xin, sem, b, fb):
            cp.start()
    spread[...] = spread_matrix(fb, n_t)
    row_t = lax.broadcasted_iota(jnp.int32, (fb * n_t, tok), 0) % n_t
    col_t = lax.broadcasted_iota(jnp.int32, (tok, fb * n_t), 1) % n_t
    nt = (((1,), (1,)), ((), ()))
    cw = 128 * GROUP
    outs = []
    for b in range(n_blocks):
        cols = pl.ds(b * fb, fb)
        rep = lax.dot_general(spread[...], codes[:, cols], (((0,), (1,)), ((), ())),
                              preferred_element_type=F32)
        for t in range(n_t):
            lhs[:, t * tok:(t + 1) * tok] = jnp.where(row_t == t, rep, 0.0).astype(BF)

        @pl.loop(0, width // cw)
        def _(g):
            at = pl.ds(pl.multiple_of(g * cw, cw), cw)
            out = jnp.dot(lhs[...], err[:, at], preferred_element_type=F32).astype(BF)
            for j in range(GROUP):
                yout.at[g * GROUP + j, cols].reshape(fb * n_t, 128)[...] = (
                    out[:, j * 128:(j + 1) * 128])

        for j in range(width // 128):
            cp = pltpu.make_async_copy(yout.at[j, cols],
                                       grad_dec.at[cols, :, pl.ds(j * 128, 128)],
                                       osem.at[b, j])
            cp.start()
            outs.append(cp)
        for cp in load_copies(dec, xin, sem, b, fb):
            cp.wait()
        gsum[...] = jnp.zeros_like(gsum)

        @pl.loop(0, width // cw)
        def _(g):
            at = pl.ds(pl.multiple_of(g * cw, cw), cw)
            gsum[...] += lax.dot_general(err[:, at], wide(xin, g * GROUP, GROUP, b, fb), nt,
                                         preferred_element_type=F32)

        own = jnp.zeros((tok, fb * n_t), F32)
        for t in range(n_t):
            own = jnp.where(col_t == t, gsum[t * tok:(t + 1) * tok, :], own)
        high = own.astype(BF)
        low = (own - high.astype(F32)).astype(BF)
        code_grad = (lax.dot_general(high, spread[...], nt, preferred_element_type=F32)
                     + lax.dot_general(low, spread[...], nt, preferred_element_type=F32))
        pre_grad = (code_grad * active[:, cols]).astype(BF)
        ebuf[:, cols] = lax.dot_general(
            feat[...], pre_grad, (((0,), (0,)), ((), ())), preferred_element_type=F32
        ).astype(BF)
        cp = pltpu.make_async_copy(ebuf.at[:, cols], grad_enc.at[:, cols], esem.at[b])
        cp.start()
        outs.append(cp)
    for cp in outs:
        cp.wait()


def grads(features, codes, active, err, dec):
    lat_dev, n_t, width = dec.shape
    tok, d_in = features.shape
    fb = 256
    n_blocks = lat_dev // fb
    vm = pl.BlockSpec(memory_space=pltpu.VMEM)
    hbm = pl.BlockSpec(memory_space=pl.ANY)
    tiles = pltpu.VMEM((width // 128, lat_dev, n_t, 128), BF)
    return pl.pallas_call(
        functools.partial(grad_kernel, fb, n_blocks),
        out_shape=(jax.ShapeDtypeStruct((d_in, lat_dev), BF),
                   jax.ShapeDtypeStruct((lat_dev, n_t, width), BF)),
        in_specs=[vm, vm, vm, vm, hbm],
        out_specs=(hbm, hbm),
        scratch_shapes=[
            tiles, tiles,
            pltpu.VMEM((n_t * tok, fb * n_t), F32),
            pltpu.VMEM((fb * n_t, n_t * tok), BF),
            pltpu.VMEM((fb, fb * n_t), BF),
            pltpu.VMEM((d_in, lat_dev), BF),
            pltpu.SemaphoreType.DMA((n_blocks, width // 128)),
            pltpu.SemaphoreType.DMA((n_blocks, width // 128)),
            pltpu.SemaphoreType.DMA((n_blocks,)),
        ],
        compiler_params=pltpu.CompilerParams(vmem_limit_bytes=58 * 2**20),
        cost_estimate=pl.CostEstimate(
            flops=18 * 10**9, bytes_accessed=2**25 + 2**22, transcendentals=0),
    )(features, codes, active, err, dec)


def per_device(inputs, targets, top_index, enc_weight, dec_weight):
    n_layer = lax.axis_size("layer")
    n_lat = lax.axis_size("lat")
    layer_count = inputs.shape[0]
    tok_count = inputs.shape[1]
    lat_dev = enc_weight.shape[1]
    per_layer = n_layer // layer_count
    layer_id = lax.axis_index("layer") // per_layer
    lat_first = (lax.axis_index("layer") % per_layer * n_lat + lax.axis_index("lat")) * lat_dev
    tuned = (per_layer == 2 and layer_count == 4 and lat_dev % 256 == 0
             and targets.shape[0] * 2 * n_lat == tok_count and targets.shape[0] % 16 == 0
             and inputs.shape[2] % 256 == 0 and dec_weight.shape[2] % 512 == 0)
    if tuned:
        chosen = lax.dynamic_index_in_dim(top_index, layer_id, 0, keepdims=False)
        ids = (lat_first + jnp.arange(lat_dev, dtype=jnp.int32))[None, :]
        errors, err_used, features, codes, active = forward_pass(
            inputs, targets, chosen, ids, enc_weight, dec_weight)
        grad_enc, grad_dec = grads(
            features, codes, active, err_used.reshape(-1, err_used.shape[2]), dec_weight)
        return (errors, grad_enc, grad_dec)
    own_part = lax.dynamic_index_in_dim(inputs, layer_id, 0, keepdims=False)
    features = lax.all_gather(own_part, "lat", axis=1, tiled=True)
    preact = jnp.dot(features, enc_weight, preferred_element_type=jnp.float32)
    chosen = lax.dynamic_index_in_dim(top_index, layer_id, 0, keepdims=False)
    lat_ids = lat_first + jnp.arange(lat_dev, dtype=jnp.int32)
    active = jnp.any(chosen[:, :, None] == lat_ids[None, None, :], axis=1).astype(jnp.float32)
    code_vals = (preact * active).astype(jnp.bfloat16)
    reach_mask = (jnp.arange(layer_count, dtype=jnp.int32) >= layer_id).astype(jnp.float32)
    width = dec_weight.shape[2]
    row_count = targets.shape[0] * lax.axis_size(("layer", "lat"))
    result = jnp.einsum("nf,ftd->tnd", code_vals, dec_weight, preferred_element_type=jnp.float32)
    result = result * reach_mask[:, None, None]
    decoded = lax.psum_scatter(
        result.reshape(row_count, width), ("layer", "lat"), scatter_dimension=0, tiled=True
    )
    errors = decoded - targets.astype(jnp.float32)
    err_b = errors.astype(jnp.bfloat16)
    all_err = lax.all_gather(err_b, ("layer", "lat"), axis=0, tiled=True)
    err_used = (
        all_err.reshape(layer_count, tok_count, width)
        * reach_mask.astype(jnp.bfloat16)[:, None, None]
    )
    code_grad = jnp.einsum("lnd,fld->nf", err_used, dec_weight, preferred_element_type=jnp.float32)
    pre_grad = (code_grad * active).astype(jnp.bfloat16)
    grad_enc = lax.dot_general(
        features, pre_grad, (((0,), (0,)), ((), ())), preferred_element_type=jnp.float32
    ).astype(jnp.bfloat16)
    grad_dec = jnp.einsum(
        "nf,lnd->fld", code_vals, err_used, preferred_element_type=jnp.float32
    ).astype(jnp.bfloat16)
    return (errors, grad_enc, grad_dec)


def solution(mesh):
    in_specs = (
        P(None, None, "lat"),
        P(("layer", "lat"), None),
        P(),
        P(None, ("layer", "lat")),
        P(("layer", "lat"), None, None),
    )
    out_specs = (
        P(("layer", "lat"), None),
        P(None, ("layer", "lat")),
        P(("layer", "lat"), None, None),
    )
    return jax.shard_map(
        per_device, mesh=mesh, in_specs=in_specs, out_specs=out_specs, check_vma=False
    )
```
